32 devices in a mesh: pipe: 2 (over core), tensor: 4 (over y, x), dp: 4 (over z).
Axes of the slice: x: 2, y: 2, z: 4, core: 2. Of those that a mesh axis runs over, the one named last changes fastest.
Arguments:
- hidden_in: bfloat16 [4, 2, 64, 8192], P(None, None, 'tensor', 'dp'), may hold values from -3 to 3
- q_weight: bfloat16 [2, 8192, 8192], P('pipe', 'dp', 'tensor'), may hold values from -0.0625 to 0.0625
- kv_weight: bfloat16 [2, 8192, 2048], P('pipe', 'dp', 'tensor'), may hold values from -0.0625 to 0.0625
- out_weight: bfloat16 [2, 8192, 8192], P('pipe', 'tensor', 'dp'), may hold values from -0.0625 to 0.0625
- gate_weight: bfloat16 [2, 8192, 14336], P('pipe', 'dp', 'tensor'), may hold values from -0.0625 to 0.0625
- up_weight: bfloat16 [2, 8192, 14336], P('pipe', 'dp', 'tensor'), may hold values from -0.0625 to 0.0625
- down_weight: bfloat16 [2, 14336, 8192], P('pipe', 'tensor', 'dp'), may hold values from -0.125 to 0.125
- key_cache: bfloat16 [2, 2, 64, 256, 1024], P('pipe', None, ('tensor', 'dp')), may hold values from -6 to 6
- value_cache: bfloat16 [2, 2, 64, 256, 1024], P('pipe', None, ('tensor', 'dp')), may hold values from -6 to 6
- block_ids: int32 [2, 4, 2, 8, 4, 3], P('pipe', None, None, None, 'tensor'), may hold values from 0 to 111, as said below
- block_counts: int32 [2, 4, 2, 8, 4], P('pipe', None, None, None, 'tensor'), may hold values from 0 to 3, as said below
Outputs:
- section_out: bfloat16 [2, 4, 2, 64, 8192], P('pipe', None, None, 'tensor', 'dp')
The draws below stay inside these ranges and needn't reach their ends.
Inputs may be any that keep to these rules, and one draw needn't show every extreme that they name: `block_ids`: entry c of the list of row block k and tensor shard t names a block of that shard, t * 28 up to (t + 1) * 28 - 1; the 3 entries of one list are distinct; entries at or past the count are padding. `block_counts`: in every row block some shard's count is 3.
All inputs are finite; a program needn't handle non-finite values.
Results may differ from the reference program's by a relative error of at most 0.023.
Values may be sent and summed in bfloat16 or wider, within the bound.
A program may use at most 192 MiB of HBM per device.

```python
import math
import jax
import jax.numpy as jnp
from jax import lax

D = 8192
HQ = 64
KVH = 8
HD = 128
FF = 14336
BLOCK = 128
CAP = 3
RB_ROWS = 8
CTX = 256
STEPS = 4
LAYERS = 2
MICRO = 2
GROUP = 64
N_TENSOR = 4


def active_lists(key):
    lead_shape = (LAYERS, STEPS, MICRO, GROUP // RB_ROWS, N_TENSOR)
    per_shard = FF // (BLOCK * N_TENSOR)
    key_scores, key_counts, key_filled = jax.random.split(key, 3)
    scores = jax.random.randint(key_scores, lead_shape + (per_shard,), 0, 1 << 20) * per_shard + jnp.arange(per_shard)
    ranked = jnp.argsort(scores, axis=-1)[..., :CAP]
    block_list = ranked + per_shard * jnp.arange(N_TENSOR)[:, None]
    list_counts = jax.random.randint(key_counts, lead_shape, 0, CAP + 1)
    filled = jax.random.randint(key_filled, lead_shape[:-1], 0, N_TENSOR)
    list_counts = jnp.where(jnp.arange(N_TENSOR) == filled[..., None], CAP, list_counts)
    return (block_list.astype(jnp.int32), list_counts.astype(jnp.int32))


def draw_block_ids(key, part):
    return active_lists(key)[0]


def draw_block_counts(key, part):
    return active_lists(key)[1]


def level_of(rng, dims, cuts, low, high):
    def one(position, parts):
        draws = jax.random.uniform(jax.random.fold_in(jax.random.fold_in(rng, 6), position), (parts,), jnp.float32, low / len(cuts), high / len(cuts))
        return jnp.repeat(jnp.exp(draws), dims[position] // parts).reshape((-1,) + (1,) * (len(dims) - position - 1))

    gain = one(*cuts[0])
    for cut in cuts[1:]:
        gain = gain * one(*cut)
    return gain


def centred(own_key, extent, width, limit, shards=(), dtype=jnp.bfloat16):
    gain = level_of(own_key, extent, shards, -0.22, 0.18) if shards else 1.0
    entries = jax.random.normal(own_key, extent, jnp.float32) * width * gain
    return jnp.minimum(jnp.maximum(entries, -limit), limit).astype(dtype)


def setup_inputs(seed: int = 0) -> dict:
    streams_of = jax.random.split(jax.random.key(seed), 12)
    return {
        "hidden_in": centred(streams_of[0], (STEPS, MICRO, GROUP, D), 0.5, 3.0, ((2, 4), (3, 4))),
        "q_weight": centred(streams_of[1], (LAYERS, D, HQ * HD), D ** -0.5, 0.0625, ((0, 2), (1, 4), (2, 4))),
        "kv_weight": centred(streams_of[2], (LAYERS, D, 2 * KVH * HD), D ** -0.5, 0.0625, ((0, 2), (1, 4), (2, 4))),
        "out_weight": centred(streams_of[3], (LAYERS, HQ * HD, D), (HQ * HD) ** -0.5, 0.0625, ((0, 2), (1, 4), (2, 4))),
        "gate_weight": centred(streams_of[4], (LAYERS, D, FF), D ** -0.5, 0.0625, ((0, 2), (1, 4), (2, 4))),
        "up_weight": centred(streams_of[5], (LAYERS, D, FF), D ** -0.5, 0.0625, ((0, 2), (1, 4), (2, 4))),
        "down_weight": centred(streams_of[6], (LAYERS, FF, D), (FF // 8) ** -0.5, 0.125, ((0, 2), (1, 4), (2, 4))),
        "key_cache": centred(streams_of[7], (LAYERS, MICRO, GROUP, CTX, KVH * HD), 1.0, 6.0, ((0, 2), (2, 16))),
        "value_cache": centred(streams_of[8], (LAYERS, MICRO, GROUP, CTX, KVH * HD), 1.0, 6.0, ((0, 2), (2, 16))),
        "block_ids": draw_block_ids(jax.random.fold_in(streams_of[11], 71), 0),
        "block_counts": draw_block_counts(jax.random.fold_in(streams_of[11], 71), 0),
    }


def attend(queries, all_keys, all_values):
    row_count = queries.shape[0]
    query_heads = queries.astype(jnp.float32).reshape(row_count, KVH, HQ // KVH, HD)
    key_heads = all_keys.astype(jnp.float32).reshape(row_count, all_keys.shape[1], KVH, HD)
    value_heads = all_values.astype(jnp.float32).reshape(row_count, all_values.shape[1], KVH, HD)
    scores = jnp.einsum('rkgd,rpkd->rkgp', query_heads, key_heads) * (1.0 / math.sqrt(HD))
    highest = lax.optimization_barrier(jnp.max(scores, axis=-1, keepdims=True))
    powers = jnp.exp(scores - highest)
    weights = (powers / lax.optimization_barrier(jnp.sum(powers, axis=-1, keepdims=True))).astype(jnp.bfloat16)
    attended = jnp.einsum('rkgp,rpkd->rkgd', weights.astype(jnp.float32), value_heads)
    return attended.reshape(row_count, HQ * HD).astype(jnp.bfloat16)

def shard_sum(operand, matrix):
    row_count = operand.shape[0]
    split_width = operand.shape[1] // N_TENSOR
    operand_split = operand.reshape(row_count, N_TENSOR, split_width).transpose(1, 0, 2)
    matrix_split = matrix.reshape(N_TENSOR, split_width, matrix.shape[1])

    def accumulate(summed_rows, pieces):
        product_term = jnp.dot(pieces[0], pieces[1], preferred_element_type=jnp.float32)
        rounded = lax.optimization_barrier(product_term.astype(jnp.bfloat16))
        return (summed_rows + rounded.astype(jnp.float32), None)
    start_rows = jnp.zeros((row_count, matrix.shape[1]), jnp.float32)
    summed_rows, _ = lax.scan(accumulate, start_rows, (operand_split, matrix_split))
    return summed_rows

def block_mask(block_list, list_counts):
    active = jnp.arange(CAP)[None, None, None, :] < list_counts[..., None]
    matches = (block_list[..., None] == jnp.arange(FF // BLOCK)[None, None, None, None, :]) & active[..., None]
    neuron_mask = lax.optimization_barrier(jnp.sum(matches.astype(jnp.float32), axis=(2, 3)))
    neuron_mask = jnp.repeat(neuron_mask, RB_ROWS, axis=1).reshape(MICRO * GROUP, FF // BLOCK)
    return jnp.repeat(neuron_mask, BLOCK, axis=1)

def reference(hidden_in, q_weight, kv_weight, out_weight, gate_weight, up_weight, down_weight, key_cache, value_cache, block_ids, block_counts):
    row_count = MICRO * GROUP
    kv_width = KVH * HD
    fresh_keys = [[] for layer_idx in range(LAYERS)]
    fresh_values = [[] for layer_idx in range(LAYERS)]
    outputs = [[] for layer_idx in range(LAYERS)]
    for step_idx in range(STEPS):
        residual = hidden_in[step_idx].reshape(row_count, D)
        for layer_idx in range(LAYERS):
            queries = jnp.dot(residual, q_weight[layer_idx], preferred_element_type=jnp.float32).astype(jnp.bfloat16)
            key_value = jnp.dot(residual, kv_weight[layer_idx], preferred_element_type=jnp.float32).astype(jnp.bfloat16)
            fresh_keys[layer_idx].append(key_value[:, :kv_width])
            fresh_values[layer_idx].append(key_value[:, kv_width:])
            all_keys = jnp.concatenate([key_cache[layer_idx].reshape(row_count, CTX, kv_width), jnp.stack(fresh_keys[layer_idx], axis=1)], axis=1)
            all_values = jnp.concatenate([value_cache[layer_idx].reshape(row_count, CTX, kv_width), jnp.stack(fresh_values[layer_idx], axis=1)], axis=1)
            attended = attend(queries, all_keys, all_values)
            middle = (residual.astype(jnp.float32) + shard_sum(attended, out_weight[layer_idx])).astype(jnp.bfloat16)
            gate_sum = jnp.dot(middle, gate_weight[layer_idx], preferred_element_type=jnp.float32)
            up_sum = jnp.dot(middle, up_weight[layer_idx], preferred_element_type=jnp.float32)
            neuron_mask = block_mask(block_ids[layer_idx, step_idx], block_counts[layer_idx, step_idx])
            activated = (jnp.maximum(gate_sum, 0.0) * up_sum * neuron_mask).astype(jnp.bfloat16)
            residual = (middle.astype(jnp.float32) + shard_sum(activated, down_weight[layer_idx])).astype(jnp.bfloat16)
            outputs[layer_idx].append(residual.reshape(MICRO, GROUP, D))
    return jnp.stack([jnp.stack(outputs[layer_idx]) for layer_idx in range(LAYERS)])
```

```python
import functools
import math

import jax
import jax.numpy as jnp
from jax import lax
from jax.experimental import pallas as pl
from jax.experimental.pallas import tpu as pltpu
from jax.sharding import PartitionSpec as P

HQ = 64
KVH = 8
HD = 128
BLOCK = 128
RB_ROWS = 8
VMEM_LIMIT = 56 * 1024 * 1024
MESH = pl.DeviceIdType.MESH


def greet(axis, n, me):
    barrier = pltpu.get_barrier_semaphore()
    for k in range(1, n):
        pl.semaphore_signal(
            barrier, inc=1, device_id={axis: lax.rem(me + k, n)}, device_id_type=MESH
        )
    pl.semaphore_wait(barrier, n - 1)


def push_all(axis, n, me, source_of, dest, send_sems, recv_sems):
    copies = []
    for k in range(1, n):
        peer = lax.rem(me + k, n)
        copy = pltpu.make_async_remote_copy(
            src_ref=source_of(peer),
            dst_ref=dest,
            send_sem=send_sems.at[k - 1],
            recv_sem=recv_sems.at[k - 1],
            device_id={axis: peer},
            device_id_type=MESH,
        )
        copy.start()
        copies.append(copy)
    return copies


def exchange_kernel(axis, n, section, split, x_ref, out_ref, send_sems, recv_sems, own_sem):
    @pl.when(lax.axis_index("pipe") == section)
    def _():
        me = lax.axis_index(axis)
        greet(axis, n, me)

        def source_of(peer):
            return x_ref.at[peer] if split else x_ref

        copies = push_all(axis, n, me, source_of, out_ref.at[me], send_sems, recv_sems)
        own = pltpu.make_async_copy(source_of(me), out_ref.at[me], own_sem)
        own.start()
        own.wait()
        for copy in copies:
            copy.wait()


def reduce_kernel(axis, n, section, mid, epilogue, x_ref, *refs):
    extra = refs[:-5]
    out_ref, held, send_sems, recv_sems, own_sem = refs[-5:]

    @pl.when(lax.axis_index("pipe") == section)
    def _():
        me = lax.axis_index(axis)
        greet(axis, n, me)

        def source_of(peer):
            return x_ref.at[:, peer] if mid else x_ref.at[peer]

        copies = push_all(axis, n, me, source_of, held.at[me], send_sems, recv_sems)
        own = pltpu.make_async_copy(source_of(me), held.at[me], own_sem)
        own.start()
        own.wait()
        for copy in copies:
            copy.wait()

        @pl.loop(0, held.shape[1])
        def _(i):
            total = held[0, i].astype(jnp.float32)
            for p in range(1, n):
                total = total + held[p, i].astype(jnp.float32)
            if epilogue == "add":
                total = total + extra[0][i].astype(jnp.float32)
            elif epilogue == "activate":
                half = total.shape[1] // 2
                total = jnp.maximum(total[:, :half], 0.0) * total[:, half:]
            out_ref[i] = total.astype(jnp.bfloat16)


def exchange(x, axis, section, split, cid):
    n = lax.axis_size(axis)
    shape = x.shape if split else (n,) + x.shape
    return pl.pallas_call(
        functools.partial(exchange_kernel, axis, n, section, split),
        out_shape=jax.ShapeDtypeStruct(shape, x.dtype),
        in_specs=[pl.BlockSpec(memory_space=pl.ANY)],
        out_specs=pl.BlockSpec(memory_space=pl.ANY),
        scratch_shapes=[
            pltpu.SemaphoreType.DMA((n - 1,)),
            pltpu.SemaphoreType.DMA((n - 1,)),
            pltpu.SemaphoreType.DMA,
        ],
        compiler_params=pltpu.CompilerParams(
            collective_id=cid, has_side_effects=True, vmem_limit_bytes=VMEM_LIMIT
        ),
    )(x)


def reduce_scatter(x, axis, section, mid, cid, epilogue=None, extra=()):
    n = lax.axis_size(axis)
    piece = (x.shape[0],) + x.shape[2:] if mid else x.shape[1:]
    width = piece[-1] // 2 if epilogue == "activate" else piece[-1]
    return pl.pallas_call(
        functools.partial(reduce_kernel, axis, n, section, mid, epilogue),
        out_shape=jax.ShapeDtypeStruct(piece[:-1] + (width,), jnp.bfloat16),
        in_specs=[pl.BlockSpec(memory_space=pl.ANY)]
        + [pl.BlockSpec(memory_space=pltpu.VMEM)] * len(extra),
        out_specs=pl.BlockSpec(memory_space=pltpu.VMEM),
        scratch_shapes=[
            pltpu.VMEM((n,) + piece, jnp.bfloat16),
            pltpu.SemaphoreType.DMA((n - 1,)),
            pltpu.SemaphoreType.DMA((n - 1,)),
            pltpu.SemaphoreType.DMA,
        ],
        compiler_params=pltpu.CompilerParams(
            collective_id=cid, has_side_effects=True, vmem_limit_bytes=VMEM_LIMIT
        ),
    )(x, *extra)


def attend_kernel(steps, q_ref, k_ref, v_ref, nk_ref, nv_ref, out_ref):
    scale = 1.0 / math.sqrt(HD)
    contract = (((1,), (1,)), ((), ()))
    for h in range(KVH):
        cols = slice(h * HD, (h + 1) * HD)
        q = q_ref[0, h]
        old = lax.dot_general(q, k_ref[0, :, cols], contract, preferred_element_type=jnp.float32)
        new = lax.dot_general(q, nk_ref[0, :, cols], contract, preferred_element_type=jnp.float32)
        old = old * scale
        step = lax.rem(lax.broadcasted_iota(jnp.int32, new.shape, 0), steps)
        position = lax.broadcasted_iota(jnp.int32, new.shape, 1)
        new = jnp.where(position <= step, new * scale, -1e30)
        highest = jnp.maximum(
            jnp.max(old, axis=-1, keepdims=True), jnp.max(new, axis=-1, keepdims=True)
        )
        old = jnp.exp(old - highest)
        new = jnp.exp(new - highest)
        total = jnp.sum(old, axis=-1, keepdims=True) + jnp.sum(new, axis=-1, keepdims=True)
        old = (old / total).astype(jnp.bfloat16)
        new = (new / total).astype(jnp.bfloat16)
        attended = jnp.dot(old, v_ref[0, :, cols], preferred_element_type=jnp.float32)
        attended += jnp.dot(new, nv_ref[0, :, cols], preferred_element_type=jnp.float32)
        out_ref[0, h] = attended.astype(jnp.bfloat16)


def attend(q, keys, values, new_keys, new_values, steps):
    def spec(x):
        return pl.BlockSpec(
            (1,) + x.shape[1:], lambda i, rank=x.ndim: (i,) + (0,) * (rank - 1)
        )

    args = (q, keys, values, new_keys, new_values)
    return pl.pallas_call(
        functools.partial(attend_kernel, steps),
        grid=(q.shape[0],),
        out_shape=jax.ShapeDtypeStruct(q.shape, jnp.bfloat16),
        in_specs=[spec(x) for x in args],
        out_specs=spec(q),
        compiler_params=pltpu.CompilerParams(vmem_limit_bytes=VMEM_LIMIT),
    )(*args)


def gate_up_kernel(tile_blocks, cap, x_ref, g_ref, u_ref, ids_ref, out_ref, total):
    tile = pl.program_id(0)

    @pl.when(tile == 0)
    def _():
        total[...] = jnp.zeros_like(total)

    for half, w_ref in enumerate((g_ref, u_ref)):
        sums = jnp.dot(x_ref[...], w_ref[...], preferred_element_type=jnp.float32)
        for c in range(cap):
            cols = slice((half * cap + c) * BLOCK, (half * cap + c + 1) * BLOCK)
            picked = total[:, cols]
            for b in range(tile_blocks):
                hit = ids_ref[c] == tile * tile_blocks + b
                picked = jnp.where(hit, sums[:, b * BLOCK : (b + 1) * BLOCK], picked)
            total[:, cols] = picked

    @pl.when(tile == pl.num_programs(0) - 1)
    def _():
        out_ref[...] = total[...].astype(jnp.bfloat16)


def gate_up(x, w_gate, w_up, ids):
    rows, depth = x.shape
    cap = ids.shape[0]
    blocks = w_gate.shape[1] // BLOCK
    tile_blocks = max(b for b in (1, 2, 4) if blocks % b == 0)
    weight_spec = pl.BlockSpec((depth, tile_blocks * BLOCK), lambda i: (0, i))
    return pl.pallas_call(
        functools.partial(gate_up_kernel, tile_blocks, cap),
        grid=(blocks // tile_blocks,),
        out_shape=jax.ShapeDtypeStruct((rows, 2 * cap * BLOCK), jnp.bfloat16),
        in_specs=[
            pl.BlockSpec((rows, depth), lambda i: (0, 0)),
            weight_spec,
            weight_spec,
            pl.BlockSpec(ids.shape, lambda i: (0, 0, 0)),
        ],
        out_specs=pl.BlockSpec((rows, 2 * cap * BLOCK), lambda i: (0, 0)),
        scratch_shapes=[pltpu.VMEM((rows, 2 * cap * BLOCK), jnp.float32)],
        compiler_params=pltpu.CompilerParams(vmem_limit_bytes=VMEM_LIMIT),
    )(x, w_gate, w_up, ids)


def down_kernel(cap, blocks, act_ref, w_ref, ids_ref, out_ref, dense):
    part = 32

    @pl.when(pl.program_id(0) == 0)
    def _():
        @pl.loop(0, dense.shape[0] // part)
        def _(i):
            rows = pl.ds(pl.multiple_of(i * part, part), part)
            ids = [ids_ref[c, rows] for c in range(cap)]
            act = [
                act_ref[rows, c * BLOCK : (c + 1) * BLOCK].astype(jnp.float32)
                for c in range(cap)
            ]
            for b in range(blocks):
                spread = jnp.zeros((part, BLOCK), jnp.float32)
                for c in range(cap):
                    spread = jnp.where(ids[c] == b, act[c], spread)
                dense[rows, b * BLOCK : (b + 1) * BLOCK] = spread.astype(jnp.bfloat16)

    out_ref[...] = jnp.dot(
        dense[...], w_ref[...], preferred_element_type=jnp.float32
    ).astype(jnp.bfloat16)


def down(act, w_down, ids):
    rows = act.shape[0]
    depth, width = w_down.shape
    tile = min(512, width)
    cap = ids.shape[0]
    return pl.pallas_call(
        functools.partial(down_kernel, cap, depth // BLOCK),
        grid=(width // tile,),
        out_shape=jax.ShapeDtypeStruct((rows, width), jnp.bfloat16),
        in_specs=[
            pl.BlockSpec(act.shape, lambda i: (0, 0)),
            pl.BlockSpec((depth, tile), lambda i: (0, i)),
            pl.BlockSpec(ids.shape, lambda i: (0, 0, 0)),
        ],
        out_specs=pl.BlockSpec((rows, tile), lambda i: (0, i)),
        scratch_shapes=[pltpu.VMEM((rows, depth), jnp.bfloat16)],
        compiler_params=pltpu.CompilerParams(vmem_limit_bytes=VMEM_LIMIT),
    )(act, w_down, ids)


def on_device(
    hidden_in,
    q_weight,
    kv_weight,
    out_weight,
    gate_weight,
    up_weight,
    down_weight,
    key_cache,
    value_cache,
    block_ids,
    block_counts,
):
    tensor_size = lax.axis_size("tensor")
    dp_size = lax.axis_size("dp")
    tensor_pos = lax.axis_index("tensor")
    pipe_pos = lax.axis_index("pipe")
    steps, micro, rows_shard, features = hidden_in.shape
    rows_att = rows_shard // dp_size
    local_rows = steps * micro * rows_shard
    piece = steps * micro * rows_att
    all_rows = local_rows * tensor_size
    q_cols = q_weight.shape[2]
    kv_cols = kv_weight.shape[2]
    kv_width = KVH * HD
    heads_local = q_cols // HD
    w_gate, w_up, w_down = gate_weight[0], up_weight[0], down_weight[0]
    local_blocks = w_gate.shape[1] // BLOCK
    cap = block_ids.shape[-1]
    ctx = key_cache.shape[3]
    cache_rows = micro * rows_att
    keys = key_cache.reshape(cache_rows, ctx, kv_width)
    values = value_cache.reshape(cache_rows, ctx, kv_width)

    listed = block_ids[0, :, :, :, 0, :] - tensor_pos * local_blocks
    counted = jnp.arange(cap) < block_counts[0, :, :, :, 0][..., None]
    listed = jnp.repeat(jnp.where(counted, listed, -1), RB_ROWS, axis=2)
    listed = listed.reshape(steps, micro, tensor_size, dp_size, rows_att, cap)
    listed = listed.transpose(5, 2, 3, 0, 1, 4).reshape(cap, all_rows, 1)
    ids = jnp.broadcast_to(listed, (cap, all_rows, BLOCK))

    def run_layer(local, section):
        base = 10 * section
        full = exchange(local, "tensor", section, False, base)
        full = full.reshape(all_rows, features)
        projected = jnp.concatenate(
            [
                jnp.dot(full, q_weight[0], preferred_element_type=jnp.float32).astype(jnp.bfloat16),
                jnp.dot(full, kv_weight[0], preferred_element_type=jnp.float32).astype(
                    jnp.bfloat16
                ),
            ],
            axis=1,
        )
        projected = reduce_scatter(
            projected.reshape(tensor_size, dp_size, piece, q_cols + kv_cols),
            "dp",
            section,
            True,
            base + 1,
        )
        arrived = exchange(projected, "tensor", section, True, base + 2)
        arrived = arrived.reshape(tensor_size, steps, micro, rows_att, q_cols + kv_cols)
        q = arrived[..., :q_cols].reshape(
            tensor_size, steps, micro, rows_att, heads_local, HD
        )
        q = q.transpose(2, 3, 0, 4, 1, 5).reshape(cache_rows, KVH, HQ // KVH * steps, HD)
        fresh = arrived[..., q_cols:].transpose(2, 3, 1, 0, 4)
        fresh = fresh.reshape(cache_rows, steps, 2 * kv_width)
        fresh = jnp.pad(fresh, ((0, 0), (0, -steps % 16), (0, 0)))
        attended = attend(
            q, keys, values, fresh[..., :kv_width], fresh[..., kv_width:], steps
        )
        attended = attended.reshape(micro, rows_att, tensor_size, heads_local, steps, HD)
        attended = attended.transpose(2, 4, 0, 1, 3, 5).reshape(tensor_size, piece, q_cols)
        returned = exchange(attended, "tensor", section, True, base + 3)
        gathered = exchange(
            returned.reshape(tensor_size * piece, q_cols), "dp", section, False, base + 4
        )
        partials = jnp.dot(
            gathered.reshape(all_rows, q_cols), out_weight[0], preferred_element_type=jnp.float32
        ).astype(jnp.bfloat16)
        middle = reduce_scatter(
            partials.reshape(dp_size, tensor_size, piece, features),
            "tensor",
            section,
            True,
            base + 5,
            "add",
            (local.reshape(dp_size, piece, features),),
        )
        middle_full = exchange(
            middle.reshape(local_rows, features), "tensor", section, False, base + 6
        )
        packed = gate_up(middle_full.reshape(all_rows, features), w_gate, w_up, ids)
        rows_dp = all_rows // dp_size
        sub = min(32, rows_dp)
        activated = reduce_scatter(
            packed.reshape(dp_size, rows_dp // sub, sub, packed.shape[1]),
            "dp",
            section,
            False,
            base + 7,
            "activate",
        )
        activated = exchange(
            activated.reshape(rows_dp, cap * BLOCK), "dp", section, False, base + 8
        )
        partials = down(activated.reshape(all_rows, cap * BLOCK), w_down, ids)
        leaving = reduce_scatter(
            partials.reshape(tensor_size, dp_size, piece, features),
            "tensor",
            section,
            False,
            base + 9,
            "add",
            (middle,),
        )
        return leaving.reshape(local_rows, features)

    local = hidden_in.reshape(steps * micro, dp_size, rows_att, features)
    local = local.transpose(1, 0, 2, 3).reshape(local_rows, features)
    sections = lax.axis_size("pipe")
    result = local
    for section in range(sections):
        leaving = run_layer(local, section)
        result = jnp.where(pipe_pos == section, leaving, result)
        if section + 1 < sections:
            local = lax.ppermute(leaving, "pipe", [(section, section + 1)])
    result = result.reshape(dp_size, steps * micro, rows_att, features).transpose(1, 0, 2, 3)
    return result.reshape(1, steps, micro, rows_shard, features)


def solution(mesh):
    placed = (
        P(None, None, "tensor", "dp"),
        P("pipe", "dp", "tensor"),
        P("pipe", "dp", "tensor"),
        P("pipe", "tensor", "dp"),
        P("pipe", "dp", "tensor"),
        P("pipe", "dp", "tensor"),
        P("pipe", "tensor", "dp"),
        P("pipe", None, ("tensor", "dp"), None, None),
        P("pipe", None, ("tensor", "dp"), None, None),
        P("pipe", None, None, None, "tensor", None),
        P("pipe", None, None, None, "tensor"),
    )
    return jax.shard_map(
        on_device,
        mesh=mesh,
        in_specs=placed,
        out_specs=P("pipe", None, None, "tensor", "dp"),
        check_vma=False,
    )
```

```python
import functools
import math

import jax
import jax.numpy as jnp
from jax import lax
from jax.experimental import pallas as pl
from jax.experimental.pallas import tpu as pltpu
from jax.sharding import PartitionSpec as P

HQ = 64
KVH = 8
HD = 128
BLOCK = 128
RB_ROWS = 8
VMEM_LIMIT = 56 * 1024 * 1024
MESH = pl.DeviceIdType.MESH


def greet(axis, n, me):
    barrier = pltpu.get_barrier_semaphore()
    for k in range(1, n):
        pl.semaphore_signal(
            barrier, inc=1, device_id={axis: lax.rem(me + k, n)}, device_id_type=MESH
        )
    pl.semaphore_wait(barrier, n - 1)


def push_all(axis, n, me, source_of, dest, send_sems, recv_sems):
    copies = []
    for k in range(1, n):
        peer = lax.rem(me + k, n)
        copy = pltpu.make_async_remote_copy(
            src_ref=source_of(peer),
            dst_ref=dest,
            send_sem=send_sems.at[k - 1],
            recv_sem=recv_sems.at[k - 1],
            device_id={axis: peer},
            device_id_type=MESH,
        )
        copy.start()
        copies.append(copy)
    return copies


def exchange_kernel(axis, n, section, split, x_ref, out_ref, send_sems, recv_sems, own_sem):
    @pl.when(lax.axis_index("pipe") == section)
    def _():
        me = lax.axis_index(axis)
        greet(axis, n, me)

        def source_of(peer):
            return x_ref.at[peer] if split else x_ref

        copies = push_all(axis, n, me, source_of, out_ref.at[me], send_sems, recv_sems)
        own = pltpu.make_async_copy(source_of(me), out_ref.at[me], own_sem)
        own.start()
        own.wait()
        for copy in copies:
            copy.wait()


def exchange(x, axis, section, split, cid):
    n = lax.axis_size(axis)
    shape = x.shape if split else (n,) + x.shape
    return pl.pallas_call(
        functools.partial(exchange_kernel, axis, n, section, split),
        out_shape=jax.ShapeDtypeStruct(shape, x.dtype),
        in_specs=[pl.BlockSpec(memory_space=pl.ANY)],
        out_specs=pl.BlockSpec(memory_space=pl.ANY),
        scratch_shapes=[
            pltpu.SemaphoreType.DMA((n - 1,)),
            pltpu.SemaphoreType.DMA((n - 1,)),
            pltpu.SemaphoreType.DMA,
        ],
        compiler_params=pltpu.CompilerParams(
            collective_id=cid, has_side_effects=True, vmem_limit_bytes=VMEM_LIMIT
        ),
    )(x)


def fused_kernel(axis_a, na, axis_b, nb, section, widths, add, mode, cap, x_ref, *refs):
    w_refs = refs[: len(widths)]
    extra = refs[len(widths) : len(widths) + add]
    scratch = refs[len(widths) + add :]
    out_ref, chunks, weight, prod, held, w_sems, sa, ra, sb, rb = scratch[:10]
    ids_ref = extra[-1] if mode != "plain" else None
    piece = held.shape[2]
    width = weight.shape[1]
    tile = max(t for t in (128, 256, 512) if width % t == 0)

    @pl.when(lax.axis_index("pipe") == section)
    def _():
        me_a = lax.axis_index(axis_a)
        me_b = lax.axis_index(axis_b)
        loads = []
        start = 0
        for i, w_ref in enumerate(w_refs):
            loads.append(
                pltpu.make_async_copy(
                    w_ref, weight.at[:, start : start + widths[i]], w_sems.at[i]
                )
            )
            start += widths[i]
        for load in loads:
            load.start()
        barrier = pltpu.get_barrier_semaphore()
        for axis, n, me in ((axis_a, na, me_a), (axis_b, nb, me_b)):
            for k in range(1, n):
                pl.semaphore_signal(
                    barrier, inc=1, device_id={axis: lax.rem(me + k, n)}, device_id_type=MESH
                )
        pl.semaphore_wait(barrier, na + nb - 2)
        gathers = push_all(axis_a, na, me_a, lambda peer: x_ref, chunks.at[me_a], sa, ra)
        for load in loads:
            load.wait()
        scatters = []
        for step in range(na):
            source = lax.rem(me_a - step + na, na)
            if step:
                gathers[step - 1].wait_recv()

            if mode == "pack":
                packed = scratch[10]
                blocks = widths[0] // BLOCK
                packed[...] = jnp.zeros_like(packed)

                @pl.loop(0, blocks)
                def _(j):
                    rows = x_ref[...] if step == 0 else chunks[source]
                    for half in range(2):
                        cols = pl.ds(pl.multiple_of((half * blocks + j) * BLOCK, BLOCK), BLOCK)
                        sums = jnp.dot(
                            rows, weight[:, cols], preferred_element_type=jnp.float32
                        )
                        for c in range(cap):
                            part = slice((half * cap + c) * BLOCK, (half * cap + c + 1) * BLOCK)
                            packed[:, part] = jnp.where(
                                ids_ref[source, c] == j, sums, packed[:, part]
                            )

                for b in range(nb):
                    prod[source, b] = packed[b * piece : (b + 1) * piece].astype(jnp.bfloat16)
            else:
                if mode == "spread":
                    dense = scratch[10]

                    @pl.loop(0, weight.shape[0] // BLOCK)
                    def _(j):
                        rows = x_ref[...] if step == 0 else chunks[source]
                        spread = jnp.zeros((rows.shape[0], BLOCK), jnp.float32)
                        for c in range(cap):
                            act = rows[:, c * BLOCK : (c + 1) * BLOCK].astype(jnp.float32)
                            spread = jnp.where(ids_ref[source, c] == j, act, spread)
                        cols = pl.ds(pl.multiple_of(j * BLOCK, BLOCK), BLOCK)
                        dense[:, cols] = spread.astype(jnp.bfloat16)

                @pl.loop(0, width // tile)
                def _(j):
                    cols = pl.ds(pl.multiple_of(j * tile, tile), tile)
                    if mode == "spread":
                        rows = scratch[10][...]
                    else:
                        rows = x_ref[...] if step == 0 else chunks[source]
                    sums = jnp.dot(rows, weight[:, cols], preferred_element_type=jnp.float32)
                    for b in range(nb):
                        prod[source, b, :, cols] = sums[b * piece : (b + 1) * piece].astype(
                            jnp.bfloat16
                        )

            for k in range(1, nb):
                peer = lax.rem(me_b + k, nb)
                copy = pltpu.make_async_remote_copy(
                    src_ref=prod.at[source, peer],
                    dst_ref=held.at[me_b, source],
                    send_sem=sb.at[step, k - 1],
                    recv_sem=rb.at[step, k - 1],
                    device_id={axis_b: peer},
                    device_id_type=MESH,
                )
                copy.start()
                scatters.append(copy)
        for copy in scatters:
            copy.wait_recv()

        @pl.loop(0, na)
        def _(i):
            total = prod[i, me_b].astype(jnp.float32)
            for k in range(1, nb):
                total = total + held[lax.rem(me_b + k, nb), i].astype(jnp.float32)
            if mode == "pack":
                span = cap * BLOCK
                total = jnp.maximum(total[:, :span], 0.0) * total[:, span:]
            elif add:
                total = total + extra[0][i].astype(jnp.float32)
            out_ref[i] = total.astype(jnp.bfloat16)

        for copy in gathers + scatters:
            copy.wait_send()


def gather_dot_scatter(x, weights, axis_a, axis_b, section, cid, extra=(), mode="plain", cap=0):
    na, nb = lax.axis_size(axis_a), lax.axis_size(axis_b)
    rows, depth = x.shape
    piece = rows // nb
    widths = tuple(w.shape[1] for w in weights)
    width = sum(widths)
    sent = 2 * cap * BLOCK if mode == "pack" else width
    given = cap * BLOCK if mode == "pack" else width
    scratch = []
    if mode == "pack":
        scratch = [pltpu.VMEM((rows, sent), jnp.float32)]
    elif mode == "spread":
        scratch = [pltpu.VMEM((rows, weights[0].shape[0]), jnp.bfloat16)]
    vmem = pl.BlockSpec(memory_space=pltpu.VMEM)
    return pl.pallas_call(
        functools.partial(fused_kernel, axis_a, na, axis_b, nb, section, widths, len(extra), mode, cap),
        out_shape=jax.ShapeDtypeStruct((na, piece, given), jnp.bfloat16),
        in_specs=[vmem]
        + [pl.BlockSpec(memory_space=pl.ANY)] * len(weights)
        + [vmem] * len(extra),
        out_specs=vmem,
        scratch_shapes=[
            pltpu.VMEM((na, rows, depth), jnp.bfloat16),
            pltpu.VMEM((weights[0].shape[0], width), jnp.bfloat16),
            pltpu.VMEM((na, nb, piece, sent), jnp.bfloat16),
            pltpu.VMEM((nb, na, piece, sent), jnp.bfloat16),
            pltpu.SemaphoreType.DMA((len(weights),)),
            pltpu.SemaphoreType.DMA((na - 1,)),
            pltpu.SemaphoreType.DMA((na - 1,)),
            pltpu.SemaphoreType.DMA((na, nb - 1)),
            pltpu.SemaphoreType.DMA((na, nb - 1)),
        ]
        + scratch,
        compiler_params=pltpu.CompilerParams(
            collective_id=cid, has_side_effects=True, vmem_limit_bytes=VMEM_LIMIT
        ),
    )(x, *weights, *extra)


def attend_kernel(steps, q_ref, k_ref, v_ref, nk_ref, nv_ref, out_ref):
    scale = 1.0 / math.sqrt(HD)
    contract = (((1,), (1,)), ((), ()))
    columns = [slice(h * HD, (h + 1) * HD) for h in range(KVH)]
    rows = q_ref.shape[2]

    def scores(k):
        return jnp.concatenate(
            [
                lax.dot_general(
                    q_ref[0, h], k[0, :, columns[h]], contract, preferred_element_type=jnp.float32
                )
                for h in range(KVH)
            ],
            axis=0,
        )

    old = scores(k_ref) * scale
    new = scores(nk_ref) * scale
    step = lax.rem(lax.broadcasted_iota(jnp.int32, new.shape, 0), steps)
    position = lax.broadcasted_iota(jnp.int32, new.shape, 1)
    new = jnp.where(position <= step, new, -1e30)
    highest = jnp.maximum(
        jnp.max(old, axis=-1, keepdims=True), jnp.max(new, axis=-1, keepdims=True)
    )
    old = jnp.exp(old - highest)
    new = jnp.exp(new - highest)
    total = jnp.sum(old, axis=-1, keepdims=True) + jnp.sum(new, axis=-1, keepdims=True)
    old = old / total
    new = new / total
    for h in range(KVH):
        part = slice(h * rows, (h + 1) * rows)
        attended = jnp.dot(
            old[part].astype(jnp.bfloat16),
            v_ref[0, :, columns[h]],
            preferred_element_type=jnp.float32,
        )
        attended += jnp.dot(
            new[part].astype(jnp.bfloat16),
            nv_ref[0, :, columns[h]],
            preferred_element_type=jnp.float32,
        )
        out_ref[0, h] = attended.astype(jnp.bfloat16)


def attend(q, keys, values, new_keys, new_values, steps):
    def spec(x):
        return pl.BlockSpec(
            (1,) + x.shape[1:], lambda i, rank=x.ndim: (i,) + (0,) * (rank - 1)
        )

    args = (q, keys, values, new_keys, new_values)
    return pl.pallas_call(
        functools.partial(attend_kernel, steps),
        grid=(q.shape[0],),
        out_shape=jax.ShapeDtypeStruct(q.shape, jnp.bfloat16),
        in_specs=[spec(x) for x in args],
        out_specs=spec(q),
        compiler_params=pltpu.CompilerParams(vmem_limit_bytes=VMEM_LIMIT),
    )(*args)


def on_device(
    hidden_in,
    q_weight,
    kv_weight,
    out_weight,
    gate_weight,
    up_weight,
    down_weight,
    key_cache,
    value_cache,
    block_ids,
    block_counts,
):
    tensor_size = lax.axis_size("tensor")
    dp_size = lax.axis_size("dp")
    tensor_pos = lax.axis_index("tensor")
    pipe_pos = lax.axis_index("pipe")
    steps, micro, rows_shard, features = hidden_in.shape
    rows_att = rows_shard // dp_size
    local_rows = steps * micro * rows_shard
    piece = steps * micro * rows_att
    all_rows = local_rows * tensor_size
    q_cols = q_weight.shape[2]
    kv_cols = kv_weight.shape[2]
    kv_width = KVH * HD
    heads_local = q_cols // HD
    w_gate, w_up, w_down = gate_weight[0], up_weight[0], down_weight[0]
    local_blocks = w_gate.shape[1] // BLOCK
    cap = block_ids.shape[-1]
    ctx = key_cache.shape[3]
    cache_rows = micro * rows_att
    keys = key_cache.reshape(cache_rows, ctx, kv_width)
    values = value_cache.reshape(cache_rows, ctx, kv_width)

    listed = block_ids[0, :, :, :, 0, :] - tensor_pos * local_blocks
    counted = jnp.arange(cap) < block_counts[0, :, :, :, 0][..., None]
    listed = jnp.repeat(jnp.where(counted, listed, -1), RB_ROWS, axis=2)
    listed = listed.reshape(steps, micro, tensor_size, dp_size, rows_att, cap)

    def spread_ids(order, lead):
        rows = listed.transpose(order).reshape(lead, all_rows // lead, cap)
        rows = rows.transpose(0, 2, 1)[..., None]
        return jnp.broadcast_to(rows, rows.shape[:-1] + (BLOCK,))

    ids_tensor = spread_ids((2, 3, 0, 1, 4, 5), tensor_size)
    ids_dp = spread_ids((3, 2, 0, 1, 4, 5), dp_size)

    def run_layer(local, section):
        base = 10 * section
        projected = gather_dot_scatter(
            local, (q_weight[0], kv_weight[0]), "tensor", "dp", section, base
        )
        arrived = exchange(projected, "tensor", section, True, base + 2)
        arrived = arrived.reshape(tensor_size, steps, micro, rows_att, q_cols + kv_cols)
        q = arrived[..., :q_cols].reshape(
            tensor_size, steps, micro, rows_att, heads_local, HD
        )
        q = q.transpose(2, 3, 0, 4, 1, 5).reshape(cache_rows, KVH, HQ // KVH * steps, HD)
        fresh = arrived[..., q_cols:].transpose(2, 3, 1, 0, 4)
        fresh = fresh.reshape(cache_rows, steps, 2 * kv_width)
        fresh = jnp.pad(fresh, ((0, 0), (0, -steps % 16), (0, 0)))
        attended = attend(
            q, keys, values, fresh[..., :kv_width], fresh[..., kv_width:], steps
        )
        attended = attended.reshape(micro, rows_att, tensor_size, heads_local, steps, HD)
        attended = attended.transpose(2, 4, 0, 1, 3, 5).reshape(tensor_size, piece, q_cols)
        returned = exchange(attended, "tensor", section, True, base + 3)
        middle = gather_dot_scatter(
            returned.reshape(tensor_size * piece, q_cols),
            (out_weight[0],),
            "dp",
            "tensor",
            section,
            base + 4,
            (local.reshape(dp_size, piece, features),),
        )
        activated = gather_dot_scatter(
            middle.reshape(local_rows, features),
            (w_gate, w_up),
            "tensor",
            "dp",
            section,
            base + 6,
            (ids_tensor,),
            "pack",
            cap,
        )
        leaving = gather_dot_scatter(
            activated.reshape(tensor_size * piece, cap * BLOCK),
            (w_down,),
            "dp",
            "tensor",
            section,
            base + 8,
            (middle, ids_dp),
            "spread",
            cap,
        )
        return leaving.reshape(local_rows, features)

    local = hidden_in.reshape(steps * micro, dp_size, rows_att, features)
    local = local.transpose(1, 0, 2, 3).reshape(local_rows, features)
    sections = lax.axis_size("pipe")
    result = local
    for section in range(sections):
        leaving = run_layer(local, section)
        result = jnp.where(pipe_pos == section, leaving, result)
        if section + 1 < sections:
            local = lax.ppermute(leaving, "pipe", [(section, section + 1)])
    result = result.reshape(dp_size, steps * micro, rows_att, features).transpose(1, 0, 2, 3)
    return result.reshape(1, steps, micro, rows_shard, features)


def solution(mesh):
    placed = (
        P(None, None, "tensor", "dp"),
        P("pipe", "dp", "tensor"),
        P("pipe", "dp", "tensor"),
        P("pipe", "tensor", "dp"),
        P("pipe", "dp", "tensor"),
        P("pipe", "dp", "tensor"),
        P("pipe", "tensor", "dp"),
        P("pipe", None, ("tensor", "dp"), None, None),
        P("pipe", None, ("tensor", "dp"), None, None),
        P("pipe", None, None, None, "tensor", None),
        P("pipe", None, None, None, "tensor"),
    )
    return jax.shard_map(
        on_device,
        mesh=mesh,
        in_specs=placed,
        out_specs=P("pipe", None, None, "tensor", "dp"),
        check_vma=False,
    )
```
